32 devices in a mesh: station: 4 (over y, x), tm: 8 (over z, core).
Axes of the slice: x: 2, y: 2, z: 4, core: 2. Of those that a mesh axis runs over, the one named last changes fastest.
Arguments:
- queries: bfloat16 [64, 256, 512], P('station', 'tm'), may hold values from -36 to 36
- grid_keys: bfloat16 [64, 256, 512], P('station', 'tm'), may hold values from -12 to 12
- values: bfloat16 [64, 256, 512], P('station', 'tm'), may hold values from -6 to 6
- glob_queries: bfloat16 [256, 512], P('tm'), may hold values from -36 to 36
- glob_keys: bfloat16 [256, 512], P('tm'), may hold values from -8.4 to 8.4
- glob_values: bfloat16 [256, 512], P('tm'), may hold values from -6 to 6
- out_weight: bfloat16 [512, 512], replicated, may hold values from -0.5 to 0.5
Outputs:
- grid_output: bfloat16 [64, 256, 512], P('station', 'tm')
- glob_output: bfloat16 [256, 512], P('tm')
The draws below stay inside these ranges and needn't reach their ends.
All inputs are finite; a program needn't handle non-finite values.
Results may differ from the reference program's by a relative error of at most 0.0052.
Values may be sent and summed in bfloat16 or wider, within the bound.
No kernel may reach another device: no remote copies, remote signals or barrier semaphores. Data moves between devices by JAX's collectives and lax.ppermute only.
A program may use at most 320 MiB of HBM per device.

```python
import math
import jax
import jax.numpy as jnp
from jax import lax

H = 8
HD = 64
D = 512
RAD = 4
G = 256
STATIONS = 64
TIMES = 256


def drawn_row(key, first_salt, second_salt, row_total, level):
    picked_row = jax.random.randint(jax.random.fold_in(key, first_salt), (), 0, row_total, dtype=jnp.int32)
    sign_bits = jax.random.randint(jax.random.fold_in(key, second_salt), (D,), 0, 2, dtype=jnp.int32)
    row_values = level * (2 * sign_bits - 1).astype(jnp.float32)
    return (picked_row, row_values)


def draw_queries(key, part):
    shape_all = (STATIONS, TIMES, D)
    result = 1.4 * jnp.clip(jax.random.normal(jax.random.fold_in(key, 3), shape_all, jnp.float32), -6.0, 6.0)
    return result.astype(jnp.bfloat16)


def draw_grid_keys(key, part):
    shape_all = (STATIONS, TIMES, D)
    result = 1.4 * jnp.clip(jax.random.normal(jax.random.fold_in(key, 5), shape_all, jnp.float32), -6.0, 6.0)
    picked_row, row_values = drawn_row(key, 21, 22, STATIONS * TIMES, 12.0)
    token_ids = jnp.arange(STATIONS * TIMES, dtype=jnp.int32).reshape(STATIONS, TIMES)
    result = jnp.where((token_ids == picked_row)[..., None], row_values, result)
    return result.astype(jnp.bfloat16)


def draw_glob_keys(key, part):
    result = 1.4 * jnp.clip(jax.random.normal(jax.random.fold_in(key, 9), (G, D), jnp.float32), -6.0, 6.0)
    picked_row, row_values = drawn_row(key, 23, 24, G, 8.375)
    glob_ids = jnp.arange(G, dtype=jnp.int32)[:, None]
    result = jnp.where(glob_ids == picked_row, row_values, result)
    return result.astype(jnp.bfloat16)


def draw_glob_queries(key, part):
    row_scale = jnp.exp(jax.random.uniform(jax.random.fold_in(key, 25), (G, H, 1), jnp.float32, math.log(1.4), math.log(5.6)))
    base = jnp.clip(jax.random.normal(jax.random.fold_in(key, 7), (G, H, HD), jnp.float32), -6.0, 6.0)
    result = (base * row_scale).reshape(G, D)
    return result.astype(jnp.bfloat16)


def levels(rng, dims, shards, low, top_value):
    gain, own = 1.0, jax.random.fold_in(rng, 6)
    for dim, parts in shards:
        heights = jnp.exp(jax.random.uniform(jax.random.fold_in(own, dim), (parts,), jnp.float32, low / len(shards), top_value / len(shards)))
        gain = gain * jnp.repeat(heights, dims[dim] // parts).reshape([-1 if axis == dim else 1 for axis in range(len(dims))])
    return gain


def centred(stream_key, dims, deviation, limit, split=(), kind=jnp.bfloat16):
    values = deviation * jax.random.normal(stream_key, dims, jnp.float32)
    if split:
        values = values * levels(stream_key, dims, split, -0.22, 0.18)
    return jnp.clip(values, -limit, limit).astype(kind)


def setup_inputs(seed: int = 0) -> dict:
    seeds = jax.random.split(jax.random.key(seed), 8)
    queries = draw_queries(jax.random.fold_in(seeds[7], 71), 0)
    grid_keys = draw_grid_keys(jax.random.fold_in(seeds[7], 71), 0)
    values = centred(seeds[2], (STATIONS, TIMES, D), 1.0, 6.0, ((0, 4), (1, 8)))
    glob_queries = draw_glob_queries(jax.random.fold_in(seeds[7], 71), 0)
    glob_keys = draw_glob_keys(jax.random.fold_in(seeds[7], 71), 0)
    glob_values = centred(seeds[5], (G, D), 1.0, 6.0, ((0, 8),))
    out_weight = centred(seeds[6], (D, D), (D // 4) ** -0.5, 0.5)
    return {"queries": queries, "grid_keys": grid_keys, "values": values, "glob_queries": glob_queries, "glob_keys": glob_keys, "glob_values": glob_values, "out_weight": out_weight}


NEG_FILL = -1e+30

def band_attend(query_band, pair_band, band_top, band_left, total_rows, total_cols, glob_k, glob_v, radius):
    query_band = query_band.astype(jnp.float32)
    pair_band = pair_band.astype(jnp.float32)
    glob_k = glob_k.astype(jnp.float32)
    glob_v = glob_v.astype(jnp.float32)
    row_count, col_count, model_width = query_band.shape
    head_count = glob_k.shape[1]
    head_size = model_width // head_count
    block_side = 2 * radius
    block_across = col_count // block_side
    block_count = 2 * block_across
    cell_count = block_side * block_side
    reach_count = 4 * cell_count
    query_blocks = query_band.reshape(2, block_side, block_across, block_side, model_width).transpose(0, 2, 1, 3, 4).reshape(block_count, cell_count, head_count, head_size)
    grid_view = pair_band.reshape(3, block_side, block_across + 1, block_side, 2 * model_width)
    stacked = jnp.stack([jnp.stack([grid_view[lower:lower + 2, :, rightward:rightward + block_across] for rightward in range(2)], 0) for lower in range(2)], 0)
    windows = stacked.transpose(2, 4, 0, 3, 1, 5, 6).reshape(block_count, reach_count, 2 * model_width)
    window_keys = windows[:, :, :model_width].reshape(block_count, reach_count, head_count, head_size)
    window_vals = windows[:, :, model_width:].reshape(block_count, reach_count, head_count, head_size)
    block_ids = jnp.arange(block_count, dtype=jnp.int32)
    block_row = band_top + block_side * (block_ids // block_across)
    block_col = band_left + block_side * (block_ids % block_across)
    query_ids = jnp.arange(cell_count, dtype=jnp.int32)
    key_ids = jnp.arange(reach_count, dtype=jnp.int32)
    query_row = block_row[:, None] + query_ids[None, :] // block_side
    query_col = block_col[:, None] + query_ids[None, :] % block_side
    key_row = block_row[:, None] + key_ids // (2 * cell_count) * block_side + key_ids // (2 * block_side) % block_side - radius
    key_col = block_col[:, None] + key_ids // block_side % 2 * block_side + key_ids % block_side - radius
    in_window = (jnp.abs(query_row[:, :, None] - key_row[:, None, :]) <= radius) & (jnp.abs(query_col[:, :, None] - key_col[:, None, :]) <= radius)
    in_window = in_window & ((key_row >= 0) & (key_row < total_rows) & (key_col >= 0) & (key_col < total_cols))[:, None, :]
    score_scale = 1.0 / math.sqrt(head_size)
    highest = lax.Precision.HIGHEST
    window_scores = jnp.einsum('bqhd,bkhd->bhqk', query_blocks, window_keys, precision=highest) * score_scale
    window_scores = jnp.where(in_window[:, None], window_scores, NEG_FILL)
    global_scores = jnp.einsum('bqhd,ghd->bhqg', query_blocks, glob_k, precision=highest) * score_scale
    top_score = jnp.maximum(lax.optimization_barrier(jnp.max(window_scores, -1)), lax.optimization_barrier(jnp.max(global_scores, -1)))[..., None]
    window_exp = jnp.exp(window_scores - top_score)
    global_exp = jnp.exp(global_scores - top_score)
    denominator = lax.optimization_barrier(jnp.sum(window_exp, -1, keepdims=True)) + lax.optimization_barrier(jnp.sum(global_exp, -1, keepdims=True))
    window_weights = lax.optimization_barrier((window_exp / denominator).astype(jnp.bfloat16)).astype(jnp.float32)
    global_weights = lax.optimization_barrier((global_exp / denominator).astype(jnp.bfloat16)).astype(jnp.float32)
    attended = jnp.einsum('bhqk,bkhd->bqhd', window_weights, window_vals, precision=highest)
    attended = attended + jnp.einsum('bhqg,ghd->bqhd', global_weights, glob_v, precision=highest)
    return attended.astype(jnp.bfloat16).reshape(block_count * cell_count, model_width)

def unblock(flat_out, row_count, col_count, radius):
    block_side = 2 * radius
    block_across = col_count // block_side
    return flat_out.reshape(2, block_across, block_side, block_side, -1).transpose(0, 2, 1, 3, 4).reshape(row_count, col_count, -1)

def fold_keys(carry, pieces):
    glob_q, score_scale = (carry[3], carry[4])
    top_score, denominator, accum = (carry[0], carry[1], carry[2])
    key_part, val_part = pieces
    scores = jnp.einsum('ghd,khd->ghk', glob_q, key_part, precision=lax.Precision.HIGHEST) * score_scale
    new_top = jnp.maximum(top_score, lax.optimization_barrier(jnp.max(scores, -1)))
    fade = jnp.exp(top_score - new_top)
    weights = jnp.exp(scores - new_top[..., None])
    denominator = denominator * fade + lax.optimization_barrier(jnp.sum(weights, -1))
    accum = accum * fade[..., None] + jnp.einsum('ghk,khd->ghd', weights, val_part, precision=lax.Precision.HIGHEST)
    return ((new_top, denominator, accum, glob_q, score_scale), None)

def reference(queries, grid_keys, values, glob_queries, glob_keys, glob_values, out_weight):
    total_rows, total_cols, model_width = queries.shape
    band_rows = 4 * RAD
    paired = jnp.concatenate([grid_keys, values], -1)
    padded = jnp.pad(paired, ((RAD, RAD), (RAD, RAD), (0, 0)))
    glob_k = glob_keys.reshape(G, H, HD)
    glob_v = glob_values.reshape(G, H, HD)

    def one_band(band_index):
        band_start = band_index * band_rows
        query_band = lax.dynamic_slice_in_dim(queries, band_start, band_rows, 0)
        pair_band = lax.dynamic_slice_in_dim(padded, band_start, band_rows + 2 * RAD, 0)
        flat_out = band_attend(query_band, pair_band, band_start, 0, total_rows, total_cols, glob_k, glob_v, RAD)
        projected = jnp.dot(flat_out, out_weight, preferred_element_type=jnp.float32).astype(jnp.bfloat16)
        return unblock(projected, band_rows, total_cols, RAD)
    grid_output = lax.map(one_band, jnp.arange(total_rows // band_rows, dtype=jnp.int32)).reshape(total_rows, total_cols, model_width)
    score_scale = jnp.float32(1.0 / math.sqrt(HD))
    glob_q = glob_queries.astype(jnp.float32).reshape(G, H, HD)
    band_count = total_rows // band_rows
    key_bands = grid_keys.astype(jnp.float32).reshape(band_count, band_rows * total_cols, H, HD)
    val_bands = values.astype(jnp.float32).reshape(band_count, band_rows * total_cols, H, HD)
    start_carry = (jnp.full((G, H), NEG_FILL, jnp.float32), jnp.zeros((G, H), jnp.float32), jnp.zeros((G, H, HD), jnp.float32), glob_q, score_scale)
    carried, unused = lax.scan(fold_keys, start_carry, (key_bands, val_bands))
    carried, unused = fold_keys(carried, (glob_keys.astype(jnp.float32).reshape(G, H, HD), glob_values.astype(jnp.float32).reshape(G, H, HD)))
    attended = (carried[2] / carried[1][..., None]).reshape(G, model_width).astype(jnp.bfloat16)
    glob_output = jnp.dot(attended, out_weight, preferred_element_type=jnp.float32).astype(jnp.bfloat16)
    return (grid_output, glob_output)
```

```python
import functools

import jax
import jax.numpy as jnp
from jax import lax
from jax.experimental import pallas as pl
from jax.experimental.pallas import tpu as pltpu
from jax.sharding import PartitionSpec as P

H = 8
HD = 64
RAD = 4
SIDE = 2 * RAD
PAIR = 2 * HD
STAT = 128
NEG_FILL = -1e30
VMEM = pltpu.VMEM
BF = jnp.bfloat16
F32 = jnp.float32


def dot_nt(a, b):
    return lax.dot_general(a, b, (((1,), (1,)), ((), ())), preferred_element_type=F32)


def dot_nn(a, b):
    return lax.dot_general(a, b, (((1,), (0,)), ((), ())), preferred_element_type=F32)


def low_half(shape):
    return lax.broadcasted_iota(jnp.int32, shape, len(shape) - 1) < HD


def head_rows(q):
    q = q * jnp.asarray(HD**-0.5, q.dtype)
    low = low_half(q.shape)
    zero = jnp.zeros_like(q)
    return jnp.concatenate([jnp.where(low, q, zero), jnp.where(low, zero, q)], 0)


def with_ones(v):
    return jnp.concatenate([v, jnp.ones_like(v)], 1)


def softmax_pair(q, keys, vals, biases, round_top=False):
    n = q.shape[0]
    rows = head_rows(q)
    scores = []
    for key, bias in zip(keys, biases):
        s = dot_nt(rows, key)
        scores.append(s if bias is None else s + bias)
    top = functools.reduce(jnp.maximum, [jnp.max(s, -1, keepdims=True) for s in scores])
    if round_top:
        top = top.astype(BF).astype(F32)
    weights = [jnp.exp(s - top).astype(BF) for s in scores]
    outs = []
    for head in range(2):
        part = slice(head * n, head * n + n)
        outs.append(
            functools.reduce(
                jnp.add, [dot_nn(w[part], with_ones(v)) for w, v in zip(weights, vals)]
            )
        )
    totals = [o[:, PAIR:] for o in outs]
    low = low_half((n, PAIR))
    attended = jnp.where(low, outs[0][:, :PAIR], outs[1][:, :PAIR]) / jnp.where(
        low, totals[0], totals[1]
    )
    return attended, (top[:n], top[n:]), totals


def partial_softmax(q, keys, vals, out_refs):
    n = q.shape[0]
    lane = lax.broadcasted_iota(jnp.int32, (n, STAT), 1)
    stats = jnp.zeros((n, STAT), F32)
    pieces = []
    for p in range(H // 2):
        cut = slice(p * PAIR, (p + 1) * PAIR)
        out, tops, totals = softmax_pair(
            q[:, cut], [k[:, cut] for k in keys], [v[:, cut] for v in vals],
            [None] * len(keys), True,
        )
        pieces.append(out.astype(BF))
        for i in range(2):
            stats = jnp.where(lane == 2 * p + i, tops[i], stats)
            stats = jnp.where(lane == H + 2 * p + i, totals[i], stats)
    full = jnp.concatenate(pieces + [stats.astype(BF)], 1)
    start = 0
    for ref in out_refs:
        ref[...] = full[start : start + ref.shape[0]]
        start += ref.shape[0]


def global_kernel(pieces, *refs):
    q = jnp.concatenate([refs[i][...] for i in range(pieces)], 0)
    ka, kb, va, vb = refs[pieces : pieces + 4]
    partial_softmax(q, [ka, kb], [va, vb], refs[pieces + 4 :])


def spread(stat_lanes):
    n = stat_lanes.shape[0]
    upper = stat_lanes.astype(BF)
    lower = (stat_lanes - upper.astype(F32)).astype(BF)
    source = lax.broadcasted_iota(jnp.int32, (STAT, H * HD), 0) - H
    target = lax.broadcasted_iota(jnp.int32, (STAT, H * HD), 1) // HD
    pick = (source == target).astype(BF)
    return dot_nn(upper, pick) + dot_nn(lower, pick)


def merge(first, second):
    width = H * HD
    lane = lax.broadcasted_iota(jnp.int32, (first.shape[0], STAT), 1)
    stats = [x[:, width:].astype(F32) for x in (first, second)]
    top = jnp.maximum(stats[0], stats[1])
    mass = [s * pltpu.roll(jnp.exp(s - top), H, 1) for s in stats]
    total = mass[0] + mass[1]
    held = (lane >= H) & (lane < 2 * H)
    safe = jnp.where(held, total, 1.0)
    shares = [spread(jnp.where(held, m, 0.0) / safe) for m in mass]
    out = first[:, :width].astype(F32) * shares[0] + second[:, :width].astype(F32) * shares[1]
    return out, jnp.where(lane < H, top, jnp.where(held, total, 0.0))


def ordered(flag_ref, index, own, other):
    mine_first = flag_ref[index] == 0
    return jnp.where(mine_first, own, other), jnp.where(mine_first, other, own)


def merge_kernel(flag_index, flags, own, other, *outs):
    a, b = own[...], other[...]
    if flag_index is not None:
        a, b = ordered(flags, flag_index, a, b)
    out, stats = merge(a, b)
    full = jnp.concatenate([out.astype(BF), stats.astype(BF)], 1)
    start = 0
    for ref in outs:
        ref[...] = full[start : start + ref.shape[0]]
        start += ref.shape[0]


def last_merge_kernel(flag_index, flags, own, other, extra, weight, out_ref):
    a, b = ordered(flags, flag_index, own[...], other[...])
    out, stats = merge(a, b)
    both = jnp.concatenate([out, stats], 1)
    out, _ = merge(both, extra[...].astype(F32))
    out_ref[...] = dot_nn(out.astype(BF), weight[...]).astype(BF)


def row_window(up, own, down, block, cols, lanes):
    rows = own.shape[0]
    first, stop = block * SIDE - RAD, block * SIDE + SIDE + RAD
    parts = []
    if first < 0:
        parts.append(up[:, cols, lanes])
    parts.append(own[max(first, 0) : min(stop, rows), cols, lanes])
    if stop > rows:
        parts.append(down[:, cols, lanes])
    return jnp.concatenate(parts, 0) if len(parts) > 1 else parts[0]


def window_bias(flags, block, blocks, wrap):
    key_cols = 3 * SIDE if wrap else 2 * SIDE
    shape = (SIDE, SIDE, 2 * SIDE, key_cols)
    n, k = SIDE * SIDE, 2 * SIDE * key_cols
    q = lax.broadcasted_iota(jnp.int32, (n, k), 0)
    key = lax.broadcasted_iota(jnp.int32, (n, k), 1)
    q_row, q_col = q // SIDE, q % SIDE
    k_row, k_col = key // key_cols, key % key_cols
    if wrap:
        q_col = jnp.where(q_col < RAD, q_col + RAD, q_col + RAD + SIDE)
    else:
        q_col = q_col + RAD
    ok = (jnp.abs(q_row + RAD - k_row) <= RAD) & (jnp.abs(q_col - k_col) <= RAD)
    if block == 0:
        ok = ok & ((k_row >= RAD) | (flags[0] != 0))
    if block == blocks - 1:
        ok = ok & ((k_row < SIDE + RAD) | (flags[1] != 0))
    if wrap:
        ok = ok & ((k_col < SIDE + RAD) | (k_col >= 2 * SIDE) | (flags[3] != 0))
        ok = ok & ((k_col < SIDE) | (k_col >= SIDE + RAD) | (flags[2] != 0))
    bias = jnp.where(ok, 0.0, NEG_FILL)
    return jnp.concatenate([bias, bias], 0)


def inner_kernel(block, blocks, own_part, *refs):
    flags, q_ref, k_ref, v_ref, halo_up, halo_down, gk_own, gk_other = refs[:8]
    rows, cols, width = q_ref.shape
    own_keys = gk_own.shape[0] // 2
    bias = window_bias(flags, block, blocks, False)
    out_ref = refs[-2] if own_part else refs[-1]
    halves = RAD
    gks, gvs = global_views(gk_own, gk_other)
    for p in range(H // 2):
        lanes = slice(p * PAIR, (p + 1) * PAIR)
        gk = jnp.concatenate([g[:, lanes] for g in gks], 0)
        gv = jnp.concatenate([g[:, lanes] for g in gvs], 0)
        for j in range(cols // SIDE - 1):
            span = slice(j * SIDE, (j + 2) * SIDE)
            keys = row_window(halo_up.at[:RAD], k_ref, halo_down.at[:RAD], block, span, lanes)
            vals = row_window(halo_up.at[RAD:], v_ref, halo_down.at[RAD:], block, span, lanes)
            q = q_ref[
                block * SIDE : (block + 1) * SIDE, j * SIDE + RAD : (j + 1) * SIDE + RAD, lanes
            ].reshape(SIDE * SIDE, PAIR)
            out, _, _ = softmax_pair(
                q, [keys.reshape(-1, PAIR), gk], [vals.reshape(-1, PAIR), gv], [bias, None]
            )
            out_ref[j, :, lanes] = out.astype(BF)
    if own_part:
        gq_ref = refs[8]
        partial_softmax(gq_ref[...], gks, gvs, [refs[-1]])


def global_views(own, other):
    keys, vals = [], []
    for ref in (own, other):
        for i in range(ref.shape[0]):
            keys.append(ref[i, 0])
            vals.append(ref[i, 1])
    return [jnp.concatenate(keys, 0)], [jnp.concatenate(vals, 0)]


def swap_halves(x):
    return pltpu.roll(x.astype(F32), RAD, 1).astype(x.dtype)


def pack_kernel(flags, k_ref, v_ref, halo_up, halo_down, outer_ref, inner_ref):
    cols = k_ref.shape[1]
    first = flags[4] == 0
    groups = []
    for span in (slice(0, SIDE), slice(cols - SIDE, cols)):
        keys = jnp.concatenate([halo_up[:RAD, span], k_ref[:, span], halo_down[:RAD, span]], 0)
        vals = jnp.concatenate([halo_up[RAD:, span], v_ref[:, span], halo_down[RAD:, span]], 0)
        groups.append((keys, swap_halves(vals)))
    low = lax.broadcasted_iota(jnp.int32, groups[0][0].shape, 1) < RAD
    left = jnp.where(low, groups[0][0], groups[0][1])
    right = jnp.where(low, groups[1][1], groups[1][0])
    outer_ref[...] = jnp.where(first, left, right)
    inner_ref[...] = jnp.where(first, right, left)


def edge_kernel(blocks, flags, q_ref, k_ref, v_ref, halo_up, halo_down, gk_own, gk_other,
                outer_ref, inner_ref, weight, *refs):
    inner_blocks, out_ref = refs[:-1], refs[-1]
    rows, cols, width = q_ref.shape
    across = cols // SIDE
    gks, gvs = global_views(gk_own, gk_other)
    first = flags[4] == 0
    outer, inner = outer_ref[...], inner_ref[...]
    right = jnp.where(first, inner, outer)
    left = jnp.where(first, outer, inner)
    low = lax.broadcasted_iota(jnp.int32, right.shape, 1) < RAD
    edge_k = jnp.where(low, right, left)
    edge_v = swap_halves(jnp.where(low, left, right))
    starts = (cols - SIDE, 0)
    for block in range(blocks):
        bias = window_bias(flags, block, blocks, True)
        band = slice(block * SIDE, block * SIDE + 2 * SIDE)
        q_rows = slice(block * SIDE, (block + 1) * SIDE)
        pieces = []
        for p in range(H // 2):
            lanes = slice(p * PAIR, (p + 1) * PAIR)
            gk, gv = gks[0][:, lanes], gvs[0][:, lanes]
            windows = []
            for half, own, edge in ((slice(0, RAD), k_ref, edge_k), (slice(RAD, 2 * RAD), v_ref, edge_v)):
                last, lead = [
                    row_window(halo_up.at[half], own, halo_down.at[half], block, slice(s, s + SIDE), lanes)
                    for s in starts
                ]
                windows.append(
                    jnp.concatenate([last, edge[band, :, lanes], lead], 1).reshape(-1, PAIR)
                )
            q = jnp.concatenate(
                [q_ref[q_rows, cols - RAD :, lanes], q_ref[q_rows, :RAD, lanes]], 1
            ).reshape(SIDE * SIDE, PAIR)
            out, _, _ = softmax_pair(
                q, [windows[0], gk], [windows[1], gv], [bias, None]
            )
            pieces.append(out.astype(BF))
        wrapped = jnp.concatenate(pieces, 1)
        done = inner_blocks[block][...].reshape((across - 1) * SIDE * SIDE, width)
        all_rows = jnp.concatenate([done, wrapped], 0)
        projected = dot_nn(all_rows, weight[...]).reshape(across, SIDE, SIDE, width)
        for j in range(across):
            before = projected[(j - 1) % across][:, RAD:]
            after = projected[j][:, :RAD]
            out_ref[q_rows, j * SIDE : (j + 1) * SIDE, :] = jnp.concatenate(
                [before, after], 1
            ).astype(BF)


def call(kernel, inputs, out_shapes, flops, flags=None):
    specs = [pl.BlockSpec(memory_space=VMEM)] * len(inputs)
    if flags is not None:
        specs = [pl.BlockSpec(memory_space=pltpu.SMEM)] + specs
        inputs = [flags, *inputs]
    return pl.pallas_call(
        kernel,
        out_shape=[jax.ShapeDtypeStruct(s, BF) for s in out_shapes],
        in_specs=specs,
        out_specs=[pl.BlockSpec(memory_space=VMEM)] * len(out_shapes),
        compiler_params=pltpu.CompilerParams(vmem_limit_bytes=48 * 2**20),
        cost_estimate=pl.CostEstimate(flops=flops, bytes_accessed=2**20, transcendentals=0),
    )(*inputs)


def body(queries, grid_keys, values, glob_queries, glob_keys, glob_values, out_weight):
    rows, cols, width = queries.shape
    tokens = rows * cols
    own = glob_queries.shape[0]
    stations, across = lax.axis_size("station"), lax.axis_size("tm")
    chips = across // 2
    payload = width + STAT
    blocks = rows // SIDE
    station, column = lax.axis_index("station"), lax.axis_index("tm")
    station_bits = [1 << b for b in range(stations.bit_length() - 1)]
    chip_bits = [1 << b for b in range(chips.bit_length() - 1)]

    def over_tm(x, mask):
        return lax.ppermute(x, "tm", [(i, i ^ mask) for i in range(across)])

    def over_station(x, mask):
        return lax.ppermute(x, "station", [(i, i ^ mask) for i in range(stations)])

    flags = jnp.stack(
        [
            station > 0,
            station < stations - 1,
            column < across - 1,
            column > 0,
            column % 2 == 1,
        ]
        + [(station & bit) > 0 for bit in station_bits]
    ).astype(jnp.int32)

    up = [(i, i + 1) for i in range(stations - 1)]
    down = [(j, i) for i, j in up]
    other_keys, other_vals = over_tm(grid_keys, 1), over_tm(values, 1)
    q_pieces = [glob_queries] + [over_tm(glob_queries, 2 * m) for m in range(1, chips)]
    halo_up = lax.ppermute(jnp.concatenate([grid_keys[rows - RAD :], values[rows - RAD :]], 0), "station", up)
    halo_down = lax.ppermute(jnp.concatenate([grid_keys[:RAD], values[:RAD]], 0), "station", down)
    kv = jnp.stack([glob_keys, glob_values])
    kv_own = jnp.stack([kv] + [over_tm(kv, 2 * m) for m in range(1, chips)])
    kv_other = over_tm(kv_own, 1)

    flat = [x.reshape(tokens, width) for x in (grid_keys, other_keys, values, other_vals)]
    half = chips * own // 2
    kept, sent = call(
        functools.partial(global_kernel, chips),
        [*q_pieces, *flat],
        [(half, payload)] * 2,
        2 * 10**9,
    )
    shared = [queries, grid_keys, values, halo_up, halo_down, kv_own, kv_other]
    inner_shape = (cols // SIDE - 1, SIDE * SIDE, width)
    first_block, extra = call(
        functools.partial(inner_kernel, 0, blocks, True),
        [*shared, glob_queries],
        [inner_shape, (own, payload)],
        2 * 10**9,
        flags,
    )
    later_blocks = [
        call(functools.partial(inner_kernel, b, blocks, False), shared, [inner_shape], 2 * 10**9, flags)[0]
        for b in range(1, blocks)
    ]
    outer, inner = call(
        pack_kernel,
        [grid_keys, values, halo_up, halo_down],
        [(rows + 2 * RAD, SIDE, width)] * 2,
        10**8,
        flags,
    )
    facing = [(i, i + 1) for i in range(1, across - 1, 2)]
    outer = lax.ppermute(outer, "tm", facing + [(j, i) for i, j in facing])
    inner = over_tm(inner, 1)
    (grid_output,) = call(
        functools.partial(edge_kernel, blocks),
        [*shared, outer, inner, out_weight, first_block, *later_blocks],
        [(rows, cols, width)],
        3 * 10**9,
        flags,
    )

    for bit in reversed(chip_bits):
        arrived = over_tm(sent, 2 * bit)
        split = [(half // 2, payload)] * 2 if bit > 1 else [(half, payload)]
        merged = call(functools.partial(merge_kernel, None), [kept, arrived], split, 10**8, flags)
        kept, sent = merged if bit > 1 else (merged[0], None)
        half //= 2
    first_flag = 5
    for i, bit in enumerate(station_bits):
        arrived = over_station(kept, bit)
        if i < len(station_bits) - 1:
            (kept,) = call(
                functools.partial(merge_kernel, first_flag + i), [kept, arrived], [(own, payload)], 10**8, flags
            )
        else:
            (glob_output,) = call(
                functools.partial(last_merge_kernel, first_flag + i),
                [kept, arrived, extra, out_weight],
                [(own, width)],
                10**8,
                flags,
            )
    return grid_output, glob_output


def solution(mesh):
    return jax.shard_map(
        body,
        mesh=mesh,
        in_specs=(
            P("station", "tm", None),
            P("station", "tm", None),
            P("station", "tm", None),
            P("tm", None),
            P("tm", None),
            P("tm", None),
            P(),
        ),
        out_specs=(P("station", "tm", None), P("tm", None)),
        check_vma=False,
    )
```

```python
import functools

import jax
import jax.numpy as jnp
from jax import lax
from jax.experimental import pallas as pl
from jax.experimental.pallas import tpu as pltpu
from jax.sharding import PartitionSpec as P

H = 8
HD = 64
RAD = 4
SIDE = 2 * RAD
PAIR = 2 * HD
STAT = 128
NEG_FILL = -1e30
VMEM_GRANT = 24 * 2**20
PACK_GRANT = 56 * 2**20
VMEM = pltpu.VMEM
BF = jnp.bfloat16
F32 = jnp.float32


def dot_nt(a, b):
    return lax.dot_general(a, b, (((1,), (1,)), ((), ())), preferred_element_type=F32)


def dot_nn(a, b):
    return lax.dot_general(a, b, (((1,), (0,)), ((), ())), preferred_element_type=F32)


def low_half(shape):
    return lax.broadcasted_iota(jnp.int32, shape, len(shape) - 1) < HD


def head_rows(q):
    q = q * jnp.asarray(HD**-0.5, q.dtype)
    low = low_half(q.shape)
    zero = jnp.zeros_like(q)
    return jnp.concatenate([jnp.where(low, q, zero), jnp.where(low, zero, q)], 0)


def with_ones(v):
    return jnp.concatenate([v, jnp.ones_like(v)], 1)


def softmax_pair(q, keys, vals, biases, round_top=False):
    n = q.shape[0]
    rows = head_rows(q)
    scores = []
    for key, bias in zip(keys, biases):
        s = dot_nt(rows, key)
        scores.append(s if bias is None else s + bias)
    top = functools.reduce(jnp.maximum, [jnp.max(s, -1, keepdims=True) for s in scores])
    if round_top:
        top = top.astype(BF).astype(F32)
    weights = [jnp.exp(s - top).astype(BF) for s in scores]
    out = functools.reduce(jnp.add, [dot_nn(w, with_ones(v)) for w, v in zip(weights, vals)])
    totals = (out[:n, PAIR:], out[n:, PAIR:])
    low = low_half((n, PAIR))
    attended = jnp.where(low, out[:n, :PAIR], out[n:, :PAIR]) / jnp.where(low, *totals)
    return attended, (top[:n], top[n:]), totals


def partial_softmax(q, keys, vals, out_refs):
    n = q.shape[0]
    lane = lax.broadcasted_iota(jnp.int32, (n, STAT), 1)
    stats = jnp.zeros((n, STAT), F32)
    pieces = []
    for p in range(H // 2):
        cut = slice(p * PAIR, (p + 1) * PAIR)
        out, tops, totals = softmax_pair(
            q[:, cut], [k[:, cut] for k in keys], [v[:, cut] for v in vals],
            [None] * len(keys), True,
        )
        pieces.append(out.astype(BF))
        for i in range(2):
            stats = jnp.where(lane == 2 * p + i, tops[i], stats)
            stats = jnp.where(lane == H + 2 * p + i, totals[i], stats)
    full = jnp.concatenate(pieces + [stats.astype(BF)], 1)
    start = 0
    for ref in out_refs:
        ref[...] = full[start : start + ref.shape[0]]
        start += ref.shape[0]


def pack_first_kernel(k_ref, v_ref, gq, gk, gv, up_ref, down_ref, glob_ref, both_ref, sems):
    last = k_ref.shape[0] - RAD
    moves = [(ref, glob_ref.at[i]) for i, ref in enumerate((gq, gk, gv))]
    for i, ref in enumerate((k_ref, v_ref)):
        rows = pl.ds(i * RAD, RAD)
        moves.append((ref.at[pl.ds(last, RAD)], up_ref.at[rows]))
        moves.append((ref.at[pl.ds(0, RAD)], down_ref.at[rows]))
        moves.append((ref, both_ref.at[i]))
    copies = [pltpu.make_async_copy(*move, sems.at[i]) for i, move in enumerate(moves)]
    for copy in copies:
        copy.start()
    for copy in copies:
        copy.wait()


def global_kernel(pieces, *refs):
    gq, gk, gv, k_ref, v_ref, facing = refs[:6]
    others, outs, kv_ref = refs[6 : pieces + 5], refs[pieces + 5 : -1], refs[-1]
    kv_ref[0, 0], kv_ref[0, 1] = gk[...], gv[...]
    for i, ref in enumerate(others):
        kv_ref[i + 1] = ref[1:]
    q = jnp.concatenate([gq[...]] + [ref[0] for ref in others], 0)
    tokens = k_ref.shape[0] * k_ref.shape[1]
    keys, vals = [
        [x.reshape(tokens, -1) for x in (own[...], facing[i])] for i, own in enumerate((k_ref, v_ref))
    ]
    partial_softmax(q, keys, vals, outs)


def spread(stats):
    upper = stats.astype(BF)
    lower = (stats - upper.astype(F32)).astype(BF)
    source = lax.broadcasted_iota(jnp.int32, (2 * STAT, H * HD), 0) % STAT - H
    target = lax.broadcasted_iota(jnp.int32, (2 * STAT, H * HD), 1) // HD
    pick = (source == target).astype(BF)
    return dot_nn(jnp.concatenate([upper, lower], 1), pick)


def merge(parts):
    width, n = H * HD, parts[0].shape[0]
    lane = lax.broadcasted_iota(jnp.int32, (n, STAT), 1)
    stats = [x[:, width:].astype(F32) for x in parts]
    top = functools.reduce(jnp.maximum, stats)
    held = (lane >= H) & (lane < 2 * H)
    mass = [jnp.where(held, s * pltpu.roll(jnp.exp(s - top), H, 1), 0.0) for s in stats]
    total = functools.reduce(jnp.add, mass)
    inverse = 1.0 / jnp.where(held, total, 1.0)
    shares = spread(jnp.concatenate([m * inverse for m in mass], 0))
    out = functools.reduce(
        jnp.add,
        [x[:, :width].astype(F32) * shares[i * n : (i + 1) * n] for i, x in enumerate(parts)],
    )
    return out, jnp.where(lane < H, top, total)


def merge_kernel(*refs):
    out, stats = merge([ref[...] for ref in refs[:-1]])
    refs[-1][...] = jnp.concatenate([out.astype(BF), stats.astype(BF)], 1)


def last_merge_kernel(first_flag, flags, *refs):
    *ins, extra, weight, out_ref = refs
    parts = [ref[...] for ref in ins]
    for b in range(len(parts).bit_length() - 1):
        swap = flags[first_flag + b] != 0
        parts = [jnp.where(swap, parts[m ^ (1 << b)], part) for m, part in enumerate(parts)]
    out, _ = merge([*parts, extra[...]])
    out_ref[...] = dot_nn(out.astype(BF), weight[...]).astype(BF)


def row_window(up, own, down, block, cols, lanes):
    rows = own.shape[0]
    first, stop = block * SIDE - RAD, block * SIDE + SIDE + RAD
    parts = []
    if first < 0:
        parts.append(up[:, cols, lanes])
    parts.append(own[max(first, 0) : min(stop, rows), cols, lanes])
    if stop > rows:
        parts.append(down[:, cols, lanes])
    return jnp.concatenate(parts, 0) if len(parts) > 1 else parts[0]


def window_bias(flags, block, blocks, wrap):
    key_cols = 3 * SIDE if wrap else 2 * SIDE
    shape = (SIDE, SIDE, 2 * SIDE, key_cols)
    n, k = SIDE * SIDE, 2 * SIDE * key_cols
    q = lax.broadcasted_iota(jnp.int32, (n, k), 0)
    key = lax.broadcasted_iota(jnp.int32, (n, k), 1)
    q_row, q_col = q // SIDE, q % SIDE
    k_row, k_col = key // key_cols, key % key_cols
    if wrap:
        q_col = jnp.where(q_col < RAD, q_col + RAD, q_col + RAD + SIDE)
    else:
        q_col = q_col + RAD
    ok = (jnp.abs(q_row + RAD - k_row) <= RAD) & (jnp.abs(q_col - k_col) <= RAD)
    if block == 0:
        ok = ok & ((k_row >= RAD) | (flags[0] != 0))
    if block == blocks - 1:
        ok = ok & ((k_row < SIDE + RAD) | (flags[1] != 0))
    if wrap:
        ok = ok & ((k_col < SIDE + RAD) | (k_col >= 2 * SIDE) | (flags[3] != 0))
        ok = ok & ((k_col < SIDE) | (k_col >= SIDE + RAD) | (flags[2] != 0))
    bias = jnp.where(ok, 0.0, NEG_FILL)
    return jnp.concatenate([bias, bias], 0)


def inner_kernel(block, blocks, own_part, *refs):
    flags, q_ref, k_ref, v_ref, halo_up, halo_down, gk_own, gk_other = refs[:8]
    rows, cols, width = q_ref.shape
    own_keys = gk_own.shape[0] // 2
    bias = window_bias(flags, block, blocks, False)
    out_ref = refs[-2] if own_part else refs[-1]
    gks, gvs = global_views(gk_own, gk_other)
    for p in range(H // 2):
        lanes = slice(p * PAIR, (p + 1) * PAIR)
        gk = jnp.concatenate([g[:, lanes] for g in gks], 0)
        gv = jnp.concatenate([g[:, lanes] for g in gvs], 0)
        for j in range(cols // SIDE - 1):
            span = slice(j * SIDE, (j + 2) * SIDE)
            keys = row_window(halo_up.at[:RAD], k_ref, halo_down.at[:RAD], block, span, lanes)
            vals = row_window(halo_up.at[RAD:], v_ref, halo_down.at[RAD:], block, span, lanes)
            q = q_ref[
                block * SIDE : (block + 1) * SIDE, j * SIDE + RAD : (j + 1) * SIDE + RAD, lanes
            ].reshape(SIDE * SIDE, PAIR)
            out, _, _ = softmax_pair(
                q, [keys.reshape(-1, PAIR), gk], [vals.reshape(-1, PAIR), gv], [bias, None]
            )
            out_ref[j, :, lanes] = out.astype(BF)
    if own_part:
        gq_ref = refs[8]
        partial_softmax(gq_ref[...], gks, gvs, [refs[-1]])


def global_views(own, other):
    keys, vals = [], []
    for ref in (own, other):
        for i in range(ref.shape[0]):
            keys.append(ref[i, 0])
            vals.append(ref[i, 1])
    return [jnp.concatenate(keys, 0)], [jnp.concatenate(vals, 0)]


def swap_halves(x):
    return pltpu.roll(x.astype(F32), RAD, 1).astype(x.dtype)


def pack_kernel(flags, k_ref, v_ref, halo_up, halo_down, outer_ref, inner_ref):
    cols = k_ref.shape[1]
    first = flags[4] == 0
    groups = []
    for span in (slice(0, SIDE), slice(cols - SIDE, cols)):
        keys = jnp.concatenate([halo_up[:RAD, span], k_ref[:, span], halo_down[:RAD, span]], 0)
        vals = jnp.concatenate([halo_up[RAD:, span], v_ref[:, span], halo_down[RAD:, span]], 0)
        groups.append((keys, swap_halves(vals)))
    low = lax.broadcasted_iota(jnp.int32, groups[0][0].shape, 1) < RAD
    left = jnp.where(low, groups[0][0], groups[0][1])
    right = jnp.where(low, groups[1][1], groups[1][0])
    outer_ref[...] = jnp.where(first, left, right)
    inner_ref[...] = jnp.where(first, right, left)


def edge_kernel(blocks, flags, q_ref, k_ref, v_ref, halo_up, halo_down, gk_own, gk_other,
                outer_ref, inner_ref, weight, *refs):
    inner_blocks, out_ref = refs[:-1], refs[-1]
    rows, cols, width = q_ref.shape
    across = cols // SIDE
    gks, gvs = global_views(gk_own, gk_other)
    first = flags[4] == 0
    outer, inner = outer_ref[...], inner_ref[...]
    right = jnp.where(first, inner, outer)
    left = jnp.where(first, outer, inner)
    low = lax.broadcasted_iota(jnp.int32, right.shape, 1) < RAD
    edge_k = jnp.where(low, right, left)
    edge_v = swap_halves(jnp.where(low, left, right))
    starts = (cols - SIDE, 0)
    for block in range(blocks):
        bias = window_bias(flags, block, blocks, True)
        band = slice(block * SIDE, block * SIDE + 2 * SIDE)
        q_rows = slice(block * SIDE, (block + 1) * SIDE)
        pieces = []
        for p in range(H // 2):
            lanes = slice(p * PAIR, (p + 1) * PAIR)
            gk, gv = gks[0][:, lanes], gvs[0][:, lanes]
            windows = []
            for half, own, edge in ((slice(0, RAD), k_ref, edge_k), (slice(RAD, 2 * RAD), v_ref, edge_v)):
                last, lead = [
                    row_window(halo_up.at[half], own, halo_down.at[half], block, slice(s, s + SIDE), lanes)
                    for s in starts
                ]
                windows.append(
                    jnp.concatenate([last, edge[band, :, lanes], lead], 1).reshape(-1, PAIR)
                )
            q = jnp.concatenate(
                [q_ref[q_rows, cols - RAD :, lanes], q_ref[q_rows, :RAD, lanes]], 1
            ).reshape(SIDE * SIDE, PAIR)
            out, _, _ = softmax_pair(
                q, [windows[0], gk], [windows[1], gv], [bias, None]
            )
            pieces.append(out.astype(BF))
        wrapped = jnp.concatenate(pieces, 1)
        done = inner_blocks[block][...].reshape((across - 1) * SIDE * SIDE, width)
        all_rows = jnp.concatenate([done, wrapped], 0)
        projected = dot_nn(all_rows, weight[...]).reshape(across, SIDE, SIDE, width)
        for j in range(across):
            before = projected[(j - 1) % across][:, RAD:]
            after = projected[j][:, :RAD]
            out_ref[q_rows, j * SIDE : (j + 1) * SIDE, :] = jnp.concatenate(
                [before, after], 1
            ).astype(BF)


def call(kernel, inputs, out_shapes, flops, flags=None):
    specs = [pl.BlockSpec(memory_space=VMEM)] * len(inputs)
    if flags is not None:
        specs = [pl.BlockSpec(memory_space=pltpu.SMEM)] + specs
        inputs = [flags, *inputs]
    return pl.pallas_call(
        kernel,
        out_shape=[jax.ShapeDtypeStruct(s, BF) for s in out_shapes],
        in_specs=specs,
        out_specs=[pl.BlockSpec(memory_space=VMEM)] * len(out_shapes),
        compiler_params=pltpu.CompilerParams(vmem_limit_bytes=VMEM_GRANT),
        cost_estimate=pl.CostEstimate(flops=flops, bytes_accessed=2**20, transcendentals=0),
    )(*inputs)


def body(queries, grid_keys, values, glob_queries, glob_keys, glob_values, out_weight):
    rows, cols, width = queries.shape
    own = glob_queries.shape[0]
    stations, across = lax.axis_size("station"), lax.axis_size("tm")
    chips = across // 2
    payload = width + STAT
    blocks = rows // SIDE
    station, column = lax.axis_index("station"), lax.axis_index("tm")
    station_bits = [1 << b for b in range(stations.bit_length() - 1)]

    def over_tm(x, mask):
        return lax.ppermute(x, "tm", [(i, i ^ mask) for i in range(across)])

    def over_station(x, mask):
        return lax.ppermute(x, "station", [(i, i ^ mask) for i in range(stations)])

    flags = jnp.stack(
        [
            station > 0,
            station < stations - 1,
            column < across - 1,
            column > 0,
            column % 2 == 1,
        ]
        + [(station & bit) > 0 for bit in station_bits]
    ).astype(jnp.int32)

    up = [(i, i + 1) for i in range(stations - 1)]
    down = [(j, i) for i, j in up]
    to_up, to_down, glob, both = pl.pallas_call(
        pack_first_kernel,
        out_shape=[
            jax.ShapeDtypeStruct(shape, BF)
            for shape in [(2 * RAD, cols, width)] * 2 + [(3, own, width), (2, rows, cols, width)]
        ],
        in_specs=[pl.BlockSpec(memory_space=pltpu.HBM)] * 5,
        out_specs=[pl.BlockSpec(memory_space=VMEM)] * 4,
        scratch_shapes=[pltpu.SemaphoreType.DMA((9,))],
        compiler_params=pltpu.CompilerParams(vmem_limit_bytes=PACK_GRANT),
        cost_estimate=pl.CostEstimate(flops=10**6, bytes_accessed=2**20, transcendentals=0),
    )(grid_keys, values, glob_queries, glob_keys, glob_values)
    halo_up = lax.ppermute(to_up, "station", up)
    halo_down = lax.ppermute(to_down, "station", down)
    facing_block = over_tm(both, 1)
    pieces = [over_tm(glob, 2 * m) for m in range(1, chips)]

    *parts, kv_own = call(
        functools.partial(global_kernel, chips),
        [glob_queries, glob_keys, glob_values, grid_keys, values, facing_block, *pieces],
        [(own, payload)] * chips + [(chips, 2, own, width)],
        2 * 10**9,
    )
    kv_other = over_tm(kv_own, 1)
    shared = [queries, grid_keys, values, halo_up, halo_down, kv_own, kv_other]
    inner_shape = (cols // SIDE - 1, SIDE * SIDE, width)
    first_block, extra = call(
        functools.partial(inner_kernel, 0, blocks, True),
        [*shared, glob_queries],
        [inner_shape, (own, payload)],
        2 * 10**9,
        flags,
    )
    later_blocks = [
        call(functools.partial(inner_kernel, b, blocks, False), shared, [inner_shape], 2 * 10**9, flags)[0]
        for b in range(1, blocks)
    ]
    outer, inner = call(
        pack_kernel,
        [grid_keys, values, halo_up, halo_down],
        [(rows + 2 * RAD, SIDE, width)] * 2,
        10**8,
        flags,
    )
    facing = [(i, i + 1) for i in range(1, across - 1, 2)]
    outer = lax.ppermute(outer, "tm", facing + [(j, i) for i, j in facing])
    inner = over_tm(inner, 1)
    (grid_output,) = call(
        functools.partial(edge_kernel, blocks),
        [*shared, outer, inner, out_weight, first_block, *later_blocks],
        [(rows, cols, width)],
        3 * 10**9,
        flags,
    )

    parts = parts[:1] + [over_tm(part, 2 * m) for m, part in enumerate(parts) if m]
    (merged,) = call(merge_kernel, parts, [(own, payload)], 10**8)
    parts = [merged] + [over_station(merged, m) for m in range(1, stations)]
    (glob_output,) = call(
        functools.partial(last_merge_kernel, 5),
        [*parts, extra, out_weight],
        [(own, width)],
        10**8,
        flags,
    )
    return grid_output, glob_output


def solution(mesh):
    return jax.shard_map(
        body,
        mesh=mesh,
        in_specs=(
            P("station", "tm", None),
            P("station", "tm", None),
            P("station", "tm", None),
            P("tm", None),
            P("tm", None),
            P("tm", None),
            P(),
        ),
        out_specs=(P("station", "tm", None), P("tm", None)),
        check_vma=False,
    )
```

```python
import functools

import jax
import jax.numpy as jnp
from jax import lax
from jax.experimental import pallas as pl
from jax.experimental.pallas import tpu as pltpu
from jax.sharding import PartitionSpec as P

H = 8
HD = 64
RAD = 4
SIDE = 2 * RAD
PAIR = 2 * HD
STAT = 128
NEG_FILL = -1e30
VMEM_GRANT = 24 * 2**20
PACK_GRANT = 56 * 2**20
VMEM = pltpu.VMEM
BF = jnp.bfloat16
F32 = jnp.float32


def dot_nt(a, b):
    return lax.dot_general(a, b, (((1,), (1,)), ((), ())), preferred_element_type=F32)


def dot_nn(a, b):
    return lax.dot_general(a, b, (((1,), (0,)), ((), ())), preferred_element_type=F32)


def low_half(shape):
    return lax.broadcasted_iota(jnp.int32, shape, len(shape) - 1) < HD


def head_rows(q):
    q = q * jnp.asarray(HD**-0.5, q.dtype)
    low = low_half(q.shape)
    zero = jnp.zeros_like(q)
    return jnp.concatenate([jnp.where(low, q, zero), jnp.where(low, zero, q)], 0)


def with_ones(v):
    return jnp.concatenate([v, jnp.ones_like(v)], 1)


def softmax_pair(q, keys, vals, biases, round_top=False):
    n = q.shape[0]
    rows = head_rows(q)
    scores = []
    for key, bias in zip(keys, biases):
        s = dot_nt(rows, key)
        scores.append(s if bias is None else s + bias)
    top = functools.reduce(jnp.maximum, [jnp.max(s, -1, keepdims=True) for s in scores])
    if round_top:
        top = top.astype(BF).astype(F32)
    weights = [jnp.exp(s - top).astype(BF) for s in scores]
    out = functools.reduce(jnp.add, [dot_nn(w, with_ones(v)) for w, v in zip(weights, vals)])
    totals = (out[:n, PAIR:], out[n:, PAIR:])
    low = low_half((n, PAIR))
    attended = jnp.where(low, out[:n, :PAIR], out[n:, :PAIR]) / jnp.where(low, *totals)
    return attended, (top[:n], top[n:]), totals


def partial_softmax(q, keys, vals, out_refs):
    n = q.shape[0]
    lane = lax.broadcasted_iota(jnp.int32, (n, STAT), 1)
    stats = jnp.zeros((n, STAT), F32)
    pieces = []
    for p in range(H // 2):
        cut = slice(p * PAIR, (p + 1) * PAIR)
        out, tops, totals = softmax_pair(
            q[:, cut], [k[:, cut] for k in keys], [v[:, cut] for v in vals],
            [None] * len(keys), True,
        )
        pieces.append(out.astype(BF))
        for i in range(2):
            stats = jnp.where(lane == 2 * p + i, tops[i], stats)
            stats = jnp.where(lane == H + 2 * p + i, totals[i], stats)
    full = jnp.concatenate(pieces + [stats.astype(BF)], 1)
    start = 0
    for ref in out_refs:
        ref[...] = full[start : start + ref.shape[0]]
        start += ref.shape[0]


def swap_halves(x):
    return pltpu.roll(x.astype(F32), RAD, 1).astype(x.dtype)


def pack_first_kernel(k_ref, v_ref, gq, gk, gv, outer_ref, glob_ref, edges, sems):
    cols = k_ref.shape[1]
    moves = [
        (ref.at[:, pl.ds(start, SIDE)], edges.at[2 * j + i])
        for j, start in enumerate((0, cols - SIDE))
        for i, ref in enumerate((k_ref, v_ref))
    ]
    moves += [(ref, glob_ref.at[i]) for i, ref in enumerate((gq, gk, gv))]
    copies = [pltpu.make_async_copy(*move, sems.at[i]) for i, move in enumerate(moves)]
    for copy in copies:
        copy.start()
    for copy in copies:
        copy.wait()
    left, right = [(edges[2 * j], swap_halves(edges[2 * j + 1])) for j in range(2)]
    low = lax.broadcasted_iota(jnp.int32, left[0].shape, 1) < RAD
    second = lax.axis_index("tm") % 2 == 1
    outer_ref[...] = jnp.where(second, jnp.where(low, right[1], right[0]), jnp.where(low, *left))


def pack_second_kernel(k_ref, v_ref, facing_k, facing_v, outer_ref, up_ref, down_ref, *edge_refs):
    rows, cols = k_ref.shape[:2]
    second = lax.axis_index("tm") % 2 == 1
    outer = outer_ref[...]
    low = lax.broadcasted_iota(jnp.int32, outer.shape, 1) < RAD
    for i, (own, facing) in enumerate(((k_ref, facing_k), (v_ref, facing_v))):
        right = jnp.where(second, outer, facing[:, :SIDE])
        left = jnp.where(second, facing[:, cols - SIDE :], outer)
        edge = jnp.where(low, right, left)
        edge_refs[i][...] = edge
        for ref, band in ((up_ref, slice(rows - RAD, rows)), (down_ref, slice(0, RAD))):
            ref[i * RAD : (i + 1) * RAD, :cols] = own[band]
            ref[i * RAD : (i + 1) * RAD, cols:] = edge[band]
        outer = swap_halves(outer)


def global_kernel(pieces, *refs):
    gq, *blocks = refs[:5]
    others, outs = refs[5 : pieces + 4], refs[pieces + 4 :]
    q = jnp.concatenate([gq[...]] + [ref[0] for ref in others], 0)
    own_k, own_v, facing_k, facing_v = [ref[...].reshape(-1, ref.shape[2]) for ref in blocks]
    partial_softmax(q, [own_k, facing_k], [own_v, facing_v], outs)


def spread(stats):
    upper = stats.astype(BF)
    lower = (stats - upper.astype(F32)).astype(BF)
    source = lax.broadcasted_iota(jnp.int32, (2 * STAT, H * HD), 0) % STAT - H
    target = lax.broadcasted_iota(jnp.int32, (2 * STAT, H * HD), 1) // HD
    pick = (source == target).astype(BF)
    return dot_nn(jnp.concatenate([upper, lower], 1), pick)


def merge(parts):
    width, n = H * HD, parts[0].shape[0]
    lane = lax.broadcasted_iota(jnp.int32, (n, STAT), 1)
    stats = [x[:, width:].astype(F32) for x in parts]
    top = functools.reduce(jnp.maximum, stats)
    held = (lane >= H) & (lane < 2 * H)
    mass = [jnp.where(held, s * pltpu.roll(jnp.exp(s - top), H, 1), 0.0) for s in stats]
    total = functools.reduce(jnp.add, mass)
    inverse = 1.0 / jnp.where(held, total, 1.0)
    shares = spread(jnp.concatenate([m * inverse for m in mass], 0))
    out = functools.reduce(
        jnp.add,
        [x[:, :width].astype(F32) * shares[i * n : (i + 1) * n] for i, x in enumerate(parts)],
    )
    return out, jnp.where(lane < H, top, total)


def merge_kernel(count, *refs):
    gk, gv, *others = refs[count:-2]
    out_ref, kv_ref = refs[-2:]
    out, stats = merge([ref[...] for ref in refs[:count]])
    out_ref[...] = jnp.concatenate([out.astype(BF), stats.astype(BF)], 1)
    kv_ref[0, 0], kv_ref[0, 1] = gk[...], gv[...]
    for i, ref in enumerate(others):
        kv_ref[i + 1] = ref[1:]


def last_merge_kernel(*refs):
    *ins, extra, weight, out_ref = refs
    parts = [ref[...].astype(F32) for ref in ins]
    for b in range(len(parts).bit_length() - 1):
        swap = lax.axis_index("station") // (1 << b) % 2 == 1
        parts = [jnp.where(swap, parts[m ^ (1 << b)], part) for m, part in enumerate(parts)]
    out, _ = merge([*parts, extra[...]])
    out_ref[...] = dot_nn(out.astype(BF), weight[...]).astype(BF)


def row_window(up, own, down, block, lanes, cols, halo_cols):
    rows = own.shape[0]
    first, stop = block * SIDE - RAD, block * SIDE + SIDE + RAD
    parts = []
    if first < 0:
        parts.append(up[:, halo_cols, lanes])
    parts.append(own[max(first, 0) : min(stop, rows), cols, lanes])
    if stop > rows:
        parts.append(down[:, halo_cols, lanes])
    return jnp.concatenate(parts, 0) if len(parts) > 1 else parts[0]


def window_bias(block, blocks, wrap):
    key_cols = 3 * SIDE if wrap else 2 * SIDE
    shape = (SIDE, SIDE, 2 * SIDE, key_cols)
    n, k = SIDE * SIDE, 2 * SIDE * key_cols
    q = lax.broadcasted_iota(jnp.int32, (n, k), 0)
    key = lax.broadcasted_iota(jnp.int32, (n, k), 1)
    q_row, q_col = q // SIDE, q % SIDE
    k_row, k_col = key // key_cols, key % key_cols
    if wrap:
        q_col = jnp.where(q_col < RAD, q_col + RAD, q_col + RAD + SIDE)
    else:
        q_col = q_col + RAD
    ok = (jnp.abs(q_row + RAD - k_row) <= RAD) & (jnp.abs(q_col - k_col) <= RAD)
    bias = jnp.where(ok, 0.0, NEG_FILL)
    station, column = lax.axis_index("station"), lax.axis_index("tm")
    outside = []
    if block == 0:
        outside.append((station == 0, k_row < RAD))
    if block == blocks - 1:
        outside.append((station == lax.axis_size("station") - 1, k_row >= SIDE + RAD))
    if wrap:
        outside.append((column == lax.axis_size("tm") - 1, (k_col >= SIDE) & (k_col < SIDE + RAD)))
        outside.append((column == 0, (k_col >= SIDE + RAD) & (k_col < 2 * SIDE)))
    for edge, where in outside:
        bias = bias + jnp.where(where, jnp.where(edge, NEG_FILL, 0.0), 0.0)
    return jnp.concatenate([bias, bias], 0)


def global_views(own, other):
    keys, vals = [], []
    for ref in (own, other):
        for i in range(ref.shape[0]):
            keys.append(ref[i, 0])
            vals.append(ref[i, 1])
    return [jnp.concatenate(keys, 0)], [jnp.concatenate(vals, 0)]


def grid_kernel(q_ref, k_ref, v_ref, halo_up, halo_down, gk_own, gk_other, edge_k, edge_v, gq, weight,
                out_ref, extra_ref):
    rows, cols, width = q_ref.shape
    blocks, across = rows // SIDE, cols // SIDE
    gks, gvs = global_views(gk_own, gk_other)
    group = slice(0, SIDE)
    beyond = slice(cols, cols + SIDE)
    for block in range(blocks):
        biases = [window_bias(block, blocks, wrap) for wrap in (False, True)]
        q_rows = slice(block * SIDE, (block + 1) * SIDE)
        done = []
        for j in range(across):
            wrap = j == across - 1
            pieces = []
            for p in range(H // 2):
                lanes = slice(p * PAIR, (p + 1) * PAIR)
                windows = []
                for i, (own, edge) in enumerate(((k_ref, edge_k), (v_ref, edge_v))):
                    up, down = [ref.at[i * RAD : (i + 1) * RAD] for ref in (halo_up, halo_down)]
                    spans = [slice(j * SIDE, (j + 2) * SIDE)]
                    if wrap:
                        spans = [slice(cols - SIDE, cols), None, group]
                    parts = [
                        row_window(up, edge, down, block, lanes, group, beyond)
                        if span is None
                        else row_window(up, own, down, block, lanes, span, span)
                        for span in spans
                    ]
                    window = jnp.concatenate(parts, 1) if wrap else parts[0]
                    windows.append(window.reshape(-1, PAIR))
                if wrap:
                    q = jnp.concatenate(
                        [q_ref[q_rows, cols - RAD :, lanes], q_ref[q_rows, :RAD, lanes]], 1
                    )
                else:
                    q = q_ref[q_rows, j * SIDE + RAD : (j + 1) * SIDE + RAD, lanes]
                out, _, _ = softmax_pair(
                    q.reshape(SIDE * SIDE, PAIR),
                    [windows[0], gks[0][:, lanes]],
                    [windows[1], gvs[0][:, lanes]],
                    [biases[wrap], None],
                )
                pieces.append(out.astype(BF))
            done.append(jnp.concatenate(pieces, 1))
        projected = dot_nn(jnp.concatenate(done, 0), weight[...]).reshape(across, SIDE, SIDE, width)
        for j in range(across):
            before = projected[(j - 1) % across][:, RAD:]
            after = projected[j][:, :RAD]
            out_ref[q_rows, j * SIDE : (j + 1) * SIDE, :] = jnp.concatenate([before, after], 1).astype(BF)
    partial_softmax(gq[...], gks, gvs, [extra_ref])


def call(kernel, inputs, out_shapes, flops):
    specs = [pl.BlockSpec(memory_space=VMEM)] * len(inputs)
    return pl.pallas_call(
        kernel,
        out_shape=[jax.ShapeDtypeStruct(s, BF) for s in out_shapes],
        in_specs=specs,
        out_specs=[pl.BlockSpec(memory_space=VMEM)] * len(out_shapes),
        compiler_params=pltpu.CompilerParams(vmem_limit_bytes=VMEM_GRANT),
        cost_estimate=pl.CostEstimate(flops=flops, bytes_accessed=2**20, transcendentals=0),
    )(*inputs)


def body(queries, grid_keys, values, glob_queries, glob_keys, glob_values, out_weight):
    rows, cols, width = queries.shape
    own = glob_queries.shape[0]
    stations, across = lax.axis_size("station"), lax.axis_size("tm")
    chips = across // 2
    payload = width + STAT

    def over_tm(x, mask):
        return lax.ppermute(x, "tm", [(i, i ^ mask) for i in range(across)])

    def over_station(x, mask):
        return lax.ppermute(x, "station", [(i, i ^ mask) for i in range(stations)])

    up = [(i, i + 1) for i in range(stations - 1)]
    down = [(j, i) for i, j in up]
    facing = [over_tm(grid_keys, 1), over_tm(values, 1)]
    outer, glob = pl.pallas_call(
        pack_first_kernel,
        out_shape=[
            jax.ShapeDtypeStruct(shape, BF)
            for shape in [(rows, SIDE, width), (3, own, width)]
        ],
        in_specs=[pl.BlockSpec(memory_space=pltpu.HBM)] * 5,
        out_specs=[pl.BlockSpec(memory_space=VMEM)] * 2,
        scratch_shapes=[VMEM((4, rows, SIDE, width), BF), pltpu.SemaphoreType.DMA((7,))],
        compiler_params=pltpu.CompilerParams(vmem_limit_bytes=PACK_GRANT),
        cost_estimate=pl.CostEstimate(flops=10**6, bytes_accessed=2**20, transcendentals=0),
    )(grid_keys, values, glob_queries, glob_keys, glob_values)
    chip_edges = [(i, i + 1) for i in range(1, across - 1, 2)]
    outer = lax.ppermute(outer, "tm", chip_edges + [(j, i) for i, j in chip_edges])
    to_up, to_down, *edges = call(
        pack_second_kernel,
        [grid_keys, values, *facing, outer],
        [(2 * RAD, cols + SIDE, width)] * 2 + [(rows, SIDE, width)] * 2,
        10**6,
    )
    halo_up = lax.ppermute(to_up, "station", up)
    halo_down = lax.ppermute(to_down, "station", down)
    pieces = [over_tm(glob, 2 * m) for m in range(1, chips)]

    parts = list(call(
        functools.partial(global_kernel, chips),
        [glob_queries, grid_keys, values, *facing, *pieces],
        [(own, payload)] * chips,
        2 * 10**9,
    ))
    parts = parts[:1] + [over_tm(part, 2 * m) for m, part in enumerate(parts) if m]
    merged, kv_own = call(
        functools.partial(merge_kernel, chips),
        [*parts, glob_keys, glob_values, *pieces],
        [(own, payload), (chips, 2, own, width)],
        10**8,
    )
    kv_other = over_tm(kv_own, 1)
    grid_output, extra = call(
        grid_kernel,
        [queries, grid_keys, values, halo_up, halo_down, kv_own, kv_other, *edges, glob_queries, out_weight],
        [(rows, cols, width), (own, payload)],
        6 * 10**9,
    )

    parts = [merged] + [over_station(merged, m) for m in range(1, stations)]
    (glob_output,) = call(
        last_merge_kernel,
        [*parts, extra, out_weight],
        [(own, width)],
        10**8,
    )
    return grid_output, glob_output


def solution(mesh):
    return jax.shard_map(
        body,
        mesh=mesh,
        in_specs=(
            P("station", "tm", None),
            P("station", "tm", None),
            P("station", "tm", None),
            P("tm", None),
            P("tm", None),
            P("tm", None),
            P(),
        ),
        out_specs=(P("station", "tm", None), P("tm", None)),
        check_vma=False,
    )
```

```python
import functools

import jax
import jax.numpy as jnp
from jax import lax
from jax.experimental import pallas as pl
from jax.experimental.pallas import tpu as pltpu
from jax.sharding import PartitionSpec as P

H = 8
HD = 64
RAD = 4
SIDE = 2 * RAD
PAIR = 2 * HD
STAT = 128
NEG_FILL = -1e30
VMEM_GRANT = 24 * 2**20
PACK_GRANT = 56 * 2**20
VMEM = pltpu.VMEM
BF = jnp.bfloat16
F32 = jnp.float32


def dot_nt(a, b):
    return lax.dot_general(a, b, (((1,), (1,)), ((), ())), preferred_element_type=F32)


def dot_nn(a, b):
    return lax.dot_general(a, b, (((1,), (0,)), ((), ())), preferred_element_type=F32)


def low_half(shape):
    return lax.broadcasted_iota(jnp.int32, shape, len(shape) - 1) < HD


def head_rows(q):
    q = q * jnp.asarray(HD**-0.5, q.dtype)
    low = low_half(q.shape)
    zero = jnp.zeros_like(q)
    return jnp.concatenate([jnp.where(low, q, zero), jnp.where(low, zero, q)], 0)


def with_ones(v):
    return jnp.concatenate([v, jnp.ones_like(v)], 1)


def softmax_pair(q, keys, vals, biases, round_top=False):
    n = q.shape[0]
    rows = head_rows(q)
    scores = []
    for key, bias in zip(keys, biases):
        s = dot_nt(rows, key)
        scores.append(s if bias is None else s + bias)
    top = functools.reduce(jnp.maximum, [jnp.max(s, -1, keepdims=True) for s in scores])
    if round_top:
        top = top.astype(BF).astype(F32)
    weights = [jnp.exp(s - top).astype(BF) for s in scores]
    out = functools.reduce(jnp.add, [dot_nn(w, with_ones(v)) for w, v in zip(weights, vals)])
    totals = (out[:n, PAIR:], out[n:, PAIR:])
    low = low_half((n, PAIR))
    attended = jnp.where(low, out[:n, :PAIR], out[n:, :PAIR]) / jnp.where(low, *totals)
    return attended, (top[:n], top[n:]), totals


def partial_softmax(q, keys, vals, out_refs):
    n = q.shape[0]
    lane = lax.broadcasted_iota(jnp.int32, (n, STAT), 1)
    stats = jnp.zeros((n, STAT), F32)
    pieces = []
    for p in range(H // 2):
        cut = slice(p * PAIR, (p + 1) * PAIR)
        out, tops, totals = softmax_pair(
            q[:, cut], [k[:, cut] for k in keys], [v[:, cut] for v in vals],
            [None] * len(keys), True,
        )
        pieces.append(out.astype(BF))
        for i in range(2):
            stats = jnp.where(lane == 2 * p + i, tops[i], stats)
            stats = jnp.where(lane == H + 2 * p + i, totals[i], stats)
    full = jnp.concatenate(pieces + [stats.astype(BF)], 1)
    start = 0
    for ref in out_refs:
        ref[...] = full[start : start + ref.shape[0]]
        start += ref.shape[0]


def swap_halves(x):
    return pltpu.roll(x.astype(F32), RAD, 1).astype(x.dtype)


def pack_first_kernel(k_ref, v_ref, gq, gk, gv, outer_ref, glob_ref, edges, sems):
    cols = k_ref.shape[1]
    moves = [
        (ref.at[:, pl.ds(start, SIDE)], edges.at[2 * j + i])
        for j, start in enumerate((0, cols - SIDE))
        for i, ref in enumerate((k_ref, v_ref))
    ]
    moves += [(ref, glob_ref.at[i]) for i, ref in enumerate((gq, gk, gv))]
    copies = [pltpu.make_async_copy(*move, sems.at[i]) for i, move in enumerate(moves)]
    for copy in copies:
        copy.start()
    for copy in copies:
        copy.wait()
    left, right = [(edges[2 * j], swap_halves(edges[2 * j + 1])) for j in range(2)]
    low = lax.broadcasted_iota(jnp.int32, left[0].shape, 1) < RAD
    second = lax.axis_index("tm") % 2 == 1
    outer_ref[...] = jnp.where(second, jnp.where(low, right[1], right[0]), jnp.where(low, *left))


def pack_second_kernel(k_ref, v_ref, facing_k, facing_v, outer_ref, up_ref, down_ref, *edge_refs):
    rows, cols = k_ref.shape[:2]
    second = lax.axis_index("tm") % 2 == 1
    outer = outer_ref[...]
    low = lax.broadcasted_iota(jnp.int32, outer.shape, 1) < RAD
    for i, (own, facing) in enumerate(((k_ref, facing_k), (v_ref, facing_v))):
        right = jnp.where(second, outer, facing[:, :SIDE])
        left = jnp.where(second, facing[:, cols - SIDE :], outer)
        edge = jnp.where(low, right, left)
        edge_refs[i][...] = edge
        for ref, band in ((up_ref, slice(rows - RAD, rows)), (down_ref, slice(0, RAD))):
            ref[i * RAD : (i + 1) * RAD, :cols] = own[band]
            ref[i * RAD : (i + 1) * RAD, cols:] = edge[band]
        outer = swap_halves(outer)


def global_kernel(count, *refs):
    blocks, queries, outs = refs[:4], refs[4 : 4 + count], refs[4 + count :]
    q = jnp.concatenate([ref[...] if len(ref.shape) == 2 else ref[0] for ref in queries], 0)
    own_k, own_v, facing_k, facing_v = [ref[...].reshape(-1, ref.shape[2]) for ref in blocks]
    partial_softmax(q, [own_k, facing_k], [own_v, facing_v], outs)


def spread(stats):
    upper = stats.astype(BF)
    lower = (stats - upper.astype(F32)).astype(BF)
    source = lax.broadcasted_iota(jnp.int32, (2 * STAT, H * HD), 0) % STAT - H
    target = lax.broadcasted_iota(jnp.int32, (2 * STAT, H * HD), 1) // HD
    pick = (source == target).astype(BF)
    return dot_nn(jnp.concatenate([upper, lower], 1), pick)


def merge(parts):
    width, n = H * HD, parts[0].shape[0]
    lane = lax.broadcasted_iota(jnp.int32, (n, STAT), 1)
    stats = [x[:, width:].astype(F32) for x in parts]
    top = functools.reduce(jnp.maximum, stats)
    held = (lane >= H) & (lane < 2 * H)
    mass = [jnp.where(held, s * pltpu.roll(jnp.exp(s - top), H, 1), 0.0) for s in stats]
    total = functools.reduce(jnp.add, mass)
    inverse = 1.0 / jnp.where(held, total, 1.0)
    shares = spread(jnp.concatenate([m * inverse for m in mass], 0))
    out = functools.reduce(
        jnp.add,
        [x[:, :width].astype(F32) * shares[i * n : (i + 1) * n] for i, x in enumerate(parts)],
    )
    return out, jnp.where(lane < H, top, total)


def merge_kernel(count, *refs):
    gk, gv, *others = refs[count:-2]
    out_ref, kv_ref = refs[-2:]
    out, stats = merge([ref[...] for ref in refs[:count]])
    out_ref[...] = jnp.concatenate([out.astype(BF), stats.astype(BF)], 1)
    kv_ref[0, 0], kv_ref[0, 1] = gk[...], gv[...]
    for i, ref in enumerate(others):
        kv_ref[i + 1] = ref[1:]


def last_merge_kernel(*refs):
    *ins, extra, weight, out_ref = refs
    parts = [ref[...].astype(F32) for ref in ins]
    for b in range(len(parts).bit_length() - 1):
        swap = lax.axis_index("station") // (1 << b) % 2 == 1
        parts = [jnp.where(swap, parts[m ^ (1 << b)], part) for m, part in enumerate(parts)]
    out, _ = merge([*parts, extra[...]])
    out_ref[...] = dot_nn(out.astype(BF), weight[...]).astype(BF)


def row_window(up, own, down, block, lanes, cols, halo_cols):
    rows = own.shape[0]
    first, stop = block * SIDE - RAD, block * SIDE + SIDE + RAD
    parts = []
    if first < 0:
        parts.append(up[:, halo_cols, lanes])
    parts.append(own[max(first, 0) : min(stop, rows), cols, lanes])
    if stop > rows:
        parts.append(down[:, halo_cols, lanes])
    return jnp.concatenate(parts, 0) if len(parts) > 1 else parts[0]


def window_bias(block, blocks, wrap):
    key_cols = 3 * SIDE if wrap else 2 * SIDE
    shape = (SIDE, SIDE, 2 * SIDE, key_cols)
    n, k = SIDE * SIDE, 2 * SIDE * key_cols
    q = lax.broadcasted_iota(jnp.int32, (n, k), 0)
    key = lax.broadcasted_iota(jnp.int32, (n, k), 1)
    q_row, q_col = q // SIDE, q % SIDE
    k_row, k_col = key // key_cols, key % key_cols
    if wrap:
        q_col = jnp.where(q_col < RAD, q_col + RAD, q_col + RAD + SIDE)
    else:
        q_col = q_col + RAD
    ok = (jnp.abs(q_row + RAD - k_row) <= RAD) & (jnp.abs(q_col - k_col) <= RAD)
    bias = jnp.where(ok, 0.0, NEG_FILL)
    station, column = lax.axis_index("station"), lax.axis_index("tm")
    outside = []
    if block == 0:
        outside.append((station == 0, k_row < RAD))
    if block == blocks - 1:
        outside.append((station == lax.axis_size("station") - 1, k_row >= SIDE + RAD))
    if wrap:
        outside.append((column == lax.axis_size("tm") - 1, (k_col >= SIDE) & (k_col < SIDE + RAD)))
        outside.append((column == 0, (k_col >= SIDE + RAD) & (k_col < 2 * SIDE)))
    for edge, where in outside:
        bias = bias + jnp.where(where, jnp.where(edge, NEG_FILL, 0.0), 0.0)
    return jnp.concatenate([bias, bias], 0)


def global_views(own, other):
    keys, vals = [], []
    for ref in (own, other):
        for i in range(ref.shape[0]):
            keys.append(ref[i, 0])
            vals.append(ref[i, 1])
    return [jnp.concatenate(keys, 0)], [jnp.concatenate(vals, 0)]


def grid_kernel(q_ref, k_ref, v_ref, halo_up, halo_down, gk_own, gk_other, edge_k, edge_v, gq, weight,
                out_ref, extra_ref):
    rows, cols, width = q_ref.shape
    blocks, across = rows // SIDE, cols // SIDE
    gks, gvs = global_views(gk_own, gk_other)
    group = slice(0, SIDE)
    beyond = slice(cols, cols + SIDE)
    for block in range(blocks):
        biases = [window_bias(block, blocks, wrap) for wrap in (False, True)]
        q_rows = slice(block * SIDE, (block + 1) * SIDE)
        done = []
        for j in range(across):
            wrap = j == across - 1
            pieces = []
            for p in range(H // 2):
                lanes = slice(p * PAIR, (p + 1) * PAIR)
                windows = []
                for i, (own, edge) in enumerate(((k_ref, edge_k), (v_ref, edge_v))):
                    up, down = [ref.at[i * RAD : (i + 1) * RAD] for ref in (halo_up, halo_down)]
                    spans = [slice(j * SIDE, (j + 2) * SIDE)]
                    if wrap:
                        spans = [slice(cols - SIDE, cols), None, group]
                    parts = [
                        row_window(up, edge, down, block, lanes, group, beyond)
                        if span is None
                        else row_window(up, own, down, block, lanes, span, span)
                        for span in spans
                    ]
                    window = jnp.concatenate(parts, 1) if wrap else parts[0]
                    windows.append(window.reshape(-1, PAIR))
                if wrap:
                    q = jnp.concatenate(
                        [q_ref[q_rows, cols - RAD :, lanes], q_ref[q_rows, :RAD, lanes]], 1
                    )
                else:
                    q = q_ref[q_rows, j * SIDE + RAD : (j + 1) * SIDE + RAD, lanes]
                out, _, _ = softmax_pair(
                    q.reshape(SIDE * SIDE, PAIR),
                    [windows[0], gks[0][:, lanes]],
                    [windows[1], gvs[0][:, lanes]],
                    [biases[wrap], None],
                )
                pieces.append(out.astype(BF))
            done.append(jnp.concatenate(pieces, 1))
        projected = dot_nn(jnp.concatenate(done, 0), weight[...]).reshape(across, SIDE, SIDE, width)
        for j in range(across):
            before = projected[(j - 1) % across][:, RAD:]
            after = projected[j][:, :RAD]
            out_ref[q_rows, j * SIDE : (j + 1) * SIDE, :] = jnp.concatenate([before, after], 1).astype(BF)
    partial_softmax(gq[...], gks, gvs, [extra_ref])


def call(kernel, inputs, out_shapes, flops):
    specs = [pl.BlockSpec(memory_space=VMEM)] * len(inputs)
    return pl.pallas_call(
        kernel,
        out_shape=[jax.ShapeDtypeStruct(s, BF) for s in out_shapes],
        in_specs=specs,
        out_specs=[pl.BlockSpec(memory_space=VMEM)] * len(out_shapes),
        compiler_params=pltpu.CompilerParams(vmem_limit_bytes=VMEM_GRANT),
        cost_estimate=pl.CostEstimate(flops=flops, bytes_accessed=2**20, transcendentals=0),
    )(*inputs)


def body(queries, grid_keys, values, glob_queries, glob_keys, glob_values, out_weight):
    rows, cols, width = queries.shape
    own = glob_queries.shape[0]
    stations, across = lax.axis_size("station"), lax.axis_size("tm")
    chips = across // 2
    payload = width + STAT

    def over_tm(x, mask):
        return lax.ppermute(x, "tm", [(i, i ^ mask) for i in range(across)])

    def over_station(x, mask):
        return lax.ppermute(x, "station", [(i, i ^ mask) for i in range(stations)])

    up = [(i, i + 1) for i in range(stations - 1)]
    down = [(j, i) for i, j in up]
    facing = [over_tm(grid_keys, 1), over_tm(values, 1)]
    outer, glob = pl.pallas_call(
        pack_first_kernel,
        out_shape=[
            jax.ShapeDtypeStruct(shape, BF)
            for shape in [(rows, SIDE, width), (3, own, width)]
        ],
        in_specs=[pl.BlockSpec(memory_space=pltpu.HBM)] * 5,
        out_specs=[pl.BlockSpec(memory_space=VMEM)] * 2,
        scratch_shapes=[VMEM((4, rows, SIDE, width), BF), pltpu.SemaphoreType.DMA((7,))],
        compiler_params=pltpu.CompilerParams(vmem_limit_bytes=PACK_GRANT),
        cost_estimate=pl.CostEstimate(flops=10**6, bytes_accessed=2**20, transcendentals=0),
    )(grid_keys, values, glob_queries, glob_keys, glob_values)
    chip_edges = [(i, i + 1) for i in range(1, across - 1, 2)]
    outer = lax.ppermute(outer, "tm", chip_edges + [(j, i) for i, j in chip_edges])
    to_up, to_down, *edges = call(
        pack_second_kernel,
        [grid_keys, values, *facing, outer],
        [(2 * RAD, cols + SIDE, width)] * 2 + [(rows, SIDE, width)] * 2,
        10**6,
    )
    halo_up = lax.ppermute(to_up, "station", up)
    halo_down = lax.ppermute(to_down, "station", down)
    pieces = [over_tm(glob, 2 * m) for m in range(1, chips)]

    parts, arrived = [], [glob_queries, *pieces]
    for some in (arrived[: chips // 2], arrived[chips // 2 :]):
        parts += call(
            functools.partial(global_kernel, len(some)),
            [grid_keys, values, *facing, *some],
            [(own, payload)] * len(some),
            10**9,
        )
    parts = parts[:1] + [over_tm(part, 2 * m) for m, part in enumerate(parts) if m]
    merged, kv_own = call(
        functools.partial(merge_kernel, chips),
        [*parts, glob_keys, glob_values, *pieces],
        [(own, payload), (chips, 2, own, width)],
        10**8,
    )
    kv_other = over_tm(kv_own, 1)
    grid_output, extra = call(
        grid_kernel,
        [queries, grid_keys, values, halo_up, halo_down, kv_own, kv_other, *edges, glob_queries, out_weight],
        [(rows, cols, width), (own, payload)],
        6 * 10**9,
    )

    parts = [merged] + [over_station(merged, m) for m in range(1, stations)]
    (glob_output,) = call(
        last_merge_kernel,
        [*parts, extra, out_weight],
        [(own, width)],
        10**8,
    )
    return grid_output, glob_output


def solution(mesh):
    return jax.shard_map(
        body,
        mesh=mesh,
        in_specs=(
            P("station", "tm", None),
            P("station", "tm", None),
            P("station", "tm", None),
            P("tm", None),
            P("tm", None),
            P("tm", None),
            P(),
        ),
        out_specs=(P("station", "tm", None), P("tm", None)),
        check_vma=False,
    )
```

```python
import functools

import jax
import jax.numpy as jnp
from jax import lax
from jax.experimental import pallas as pl
from jax.experimental.pallas import tpu as pltpu
from jax.sharding import PartitionSpec as P

H = 8
HD = 64
RAD = 4
SIDE = 2 * RAD
PAIR = 2 * HD
STAT = 128
NEG_FILL = -1e30
VMEM_GRANT = 24 * 2**20
PACK_GRANT = 56 * 2**20
VMEM = pltpu.VMEM
BF = jnp.bfloat16
F32 = jnp.float32


def dot_nt(a, b):
    return lax.dot_general(a, b, (((1,), (1,)), ((), ())), preferred_element_type=F32)


def dot_nn(a, b):
    return lax.dot_general(a, b, (((1,), (0,)), ((), ())), preferred_element_type=F32)


def low_half(shape):
    return lax.broadcasted_iota(jnp.int32, shape, len(shape) - 1) < HD


def head_rows(q):
    q = q * jnp.asarray(HD**-0.5, q.dtype)
    low = low_half(q.shape)
    zero = jnp.zeros_like(q)
    return jnp.concatenate([jnp.where(low, q, zero), jnp.where(low, zero, q)], 0)


def with_ones(v):
    return jnp.concatenate([v, jnp.ones_like(v)], 1)


def softmax_pair(q, keys, vals, biases, round_top=False):
    n = q.shape[0]
    rows = head_rows(q)
    scores = []
    for key, bias in zip(keys, biases):
        s = dot_nt(rows, key)
        scores.append(s if bias is None else s + bias)
    top = functools.reduce(jnp.maximum, [jnp.max(s, -1, keepdims=True) for s in scores])
    if round_top:
        top = top.astype(BF).astype(F32)
    weights = [jnp.exp(s - top).astype(BF) for s in scores]
    out = functools.reduce(jnp.add, [dot_nn(w, with_ones(v)) for w, v in zip(weights, vals)])
    totals = (out[:n, PAIR:], out[n:, PAIR:])
    low = low_half((n, PAIR))
    attended = jnp.where(low, out[:n, :PAIR], out[n:, :PAIR]) / jnp.where(low, *totals)
    return attended, (top[:n], top[n:]), totals


def partial_softmax(q, keys, vals, out_refs):
    n = q.shape[0]
    lane = lax.broadcasted_iota(jnp.int32, (n, STAT), 1)
    stats = jnp.zeros((n, STAT), F32)
    pieces = []
    for p in range(H // 2):
        cut = slice(p * PAIR, (p + 1) * PAIR)
        out, tops, totals = softmax_pair(
            q[:, cut], [k[:, cut] for k in keys], [v[:, cut] for v in vals],
            [None] * len(keys), True,
        )
        pieces.append(out.astype(BF))
        for i in range(2):
            stats = jnp.where(lane == 2 * p + i, tops[i], stats)
            stats = jnp.where(lane == H + 2 * p + i, totals[i], stats)
    full = jnp.concatenate(pieces + [stats.astype(BF)], 1)
    start = 0
    for ref in out_refs:
        ref[...] = full[start : start + ref.shape[0]]
        start += ref.shape[0]


def swap_halves(x):
    return pltpu.roll(x.astype(F32), RAD, 1).astype(x.dtype)


def pack_first_kernel(k_ref, v_ref, gq, gk, gv, outer_ref, glob_ref, edges, sems):
    cols = k_ref.shape[1]
    moves = [
        (ref.at[:, pl.ds(start, SIDE)], edges.at[2 * j + i])
        for j, start in enumerate((0, cols - SIDE))
        for i, ref in enumerate((k_ref, v_ref))
    ]
    moves += [(ref, glob_ref.at[i]) for i, ref in enumerate((gq, gk, gv))]
    copies = [pltpu.make_async_copy(*move, sems.at[i]) for i, move in enumerate(moves)]
    for copy in copies:
        copy.start()
    for copy in copies:
        copy.wait()
    left, right = [(edges[2 * j], swap_halves(edges[2 * j + 1])) for j in range(2)]
    low = lax.broadcasted_iota(jnp.int32, left[0].shape, 1) < RAD
    second = lax.axis_index("tm") % 2 == 1
    outer_ref[...] = jnp.where(second, jnp.where(low, right[1], right[0]), jnp.where(low, *left))


def pack_second_kernel(k_ref, v_ref, facing_k, facing_v, outer_ref, up_ref, down_ref, *edge_refs):
    rows, cols = k_ref.shape[:2]
    second = lax.axis_index("tm") % 2 == 1
    outer = outer_ref[...]
    low = lax.broadcasted_iota(jnp.int32, outer.shape, 1) < RAD
    for i, (own, facing) in enumerate(((k_ref, facing_k), (v_ref, facing_v))):
        right = jnp.where(second, outer, facing[:, :SIDE])
        left = jnp.where(second, facing[:, cols - SIDE :], outer)
        edge = jnp.where(low, right, left)
        edge_refs[i][...] = edge
        for ref, band in ((up_ref, slice(rows - RAD, rows)), (down_ref, slice(0, RAD))):
            ref[i * RAD : (i + 1) * RAD, :cols] = own[band]
            ref[i * RAD : (i + 1) * RAD, cols:] = edge[band]
        outer = swap_halves(outer)


def global_kernel(count, *refs):
    blocks, queries, outs = refs[:4], refs[4 : 4 + count], refs[4 + count :]
    q = jnp.concatenate([ref[...] if len(ref.shape) == 2 else ref[0] for ref in queries], 0)
    own_k, own_v, facing_k, facing_v = [ref[...].reshape(-1, ref.shape[2]) for ref in blocks]
    partial_softmax(q, [own_k, facing_k], [own_v, facing_v], outs)


def spread(stats):
    upper = stats.astype(BF)
    lower = (stats - upper.astype(F32)).astype(BF)
    source = lax.broadcasted_iota(jnp.int32, (2 * STAT, H * HD), 0) % STAT - H
    target = lax.broadcasted_iota(jnp.int32, (2 * STAT, H * HD), 1) // HD
    pick = (source == target).astype(BF)
    return dot_nn(jnp.concatenate([upper, lower], 1), pick)


def merge(parts):
    width, n = H * HD, parts[0].shape[0]
    lane = lax.broadcasted_iota(jnp.int32, (n, STAT), 1)
    stats = [x[:, width:].astype(F32) for x in parts]
    top = functools.reduce(jnp.maximum, stats)
    held = (lane >= H) & (lane < 2 * H)
    mass = [jnp.where(held, s * pltpu.roll(jnp.exp(s - top), H, 1), 0.0) for s in stats]
    total = functools.reduce(jnp.add, mass)
    inverse = 1.0 / jnp.where(held, total, 1.0)
    shares = spread(jnp.concatenate([m * inverse for m in mass], 0))
    out = functools.reduce(
        jnp.add,
        [x[:, :width].astype(F32) * shares[i * n : (i + 1) * n] for i, x in enumerate(parts)],
    )
    return out, jnp.where(lane < H, top, total)


def merge_kernel(count, *refs):
    gk, gv, *others = refs[count:-2]
    out_ref, kv_ref = refs[-2:]
    out, stats = merge([ref[...] for ref in refs[:count]])
    out_ref[...] = jnp.concatenate([out.astype(BF), stats.astype(BF)], 1)
    kv_ref[0, 0], kv_ref[0, 1] = gk[...], gv[...]
    for i, ref in enumerate(others):
        kv_ref[i + 1] = ref[1:]


def last_merge_kernel(*refs):
    *ins, extra, weight, out_ref = refs
    parts = [ref[...].astype(F32) for ref in ins]
    for b in range(len(parts).bit_length() - 1):
        swap = lax.axis_index("station") // (1 << b) % 2 == 1
        parts = [jnp.where(swap, parts[m ^ (1 << b)], part) for m, part in enumerate(parts)]
    out, _ = merge([*parts, extra[...]])
    out_ref[...] = dot_nn(out.astype(BF), weight[...]).astype(BF)


def row_window(up, own, down, block, lanes, cols, halo_cols):
    rows = own.shape[0]
    first, stop = block * SIDE - RAD, block * SIDE + SIDE + RAD
    parts = []
    if first < 0:
        parts.append(up[:, halo_cols, lanes])
    parts.append(own[max(first, 0) : min(stop, rows), cols, lanes])
    if stop > rows:
        parts.append(down[:, halo_cols, lanes])
    return jnp.concatenate(parts, 0) if len(parts) > 1 else parts[0]


def window_bias(block, blocks, wrap):
    key_cols = 3 * SIDE if wrap else 2 * SIDE
    shape = (SIDE, SIDE, 2 * SIDE, key_cols)
    n, k = SIDE * SIDE, 2 * SIDE * key_cols
    q = lax.broadcasted_iota(jnp.int32, (n, k), 0)
    key = lax.broadcasted_iota(jnp.int32, (n, k), 1)
    q_row, q_col = q // SIDE, q % SIDE
    k_row, k_col = key // key_cols, key % key_cols
    if wrap:
        q_col = jnp.where(q_col < RAD, q_col + RAD, q_col + RAD + SIDE)
    else:
        q_col = q_col + RAD
    ok = (jnp.abs(q_row + RAD - k_row) <= RAD) & (jnp.abs(q_col - k_col) <= RAD)
    bias = jnp.where(ok, 0.0, NEG_FILL)
    station, column = lax.axis_index("station"), lax.axis_index("tm")
    outside = []
    if block == 0:
        outside.append((station == 0, k_row < RAD))
    if block == blocks - 1:
        outside.append((station == lax.axis_size("station") - 1, k_row >= SIDE + RAD))
    if wrap:
        outside.append((column == lax.axis_size("tm") - 1, (k_col >= SIDE) & (k_col < SIDE + RAD)))
        outside.append((column == 0, (k_col >= SIDE + RAD) & (k_col < 2 * SIDE)))
    for edge, where in outside:
        bias = bias + jnp.where(where, jnp.where(edge, NEG_FILL, 0.0), 0.0)
    return jnp.concatenate([bias, bias], 0)


def global_views(own, other):
    keys, vals = [], []
    for ref in (own, other):
        for i in range(ref.shape[0]):
            keys.append(ref[i, 0])
            vals.append(ref[i, 1])
    return [jnp.concatenate(keys, 0)], [jnp.concatenate(vals, 0)]


def grid_kernel(q_ref, k_ref, v_ref, halo_up, halo_down, gk_own, gk_other, edge_k, edge_v, gq, weight,
                out_ref, extra_ref, rows_ref, sems):
    rows, cols, width = q_ref.shape
    blocks, across = rows // SIDE, cols // SIDE
    gks, gvs = global_views(gk_own, gk_other)
    group = slice(0, SIDE)
    beyond = slice(cols, cols + SIDE)
    copies = []
    for block in range(blocks):
        biases = [window_bias(block, blocks, wrap) for wrap in (False, True)]
        q_rows = slice(block * SIDE, (block + 1) * SIDE)
        done = []
        for j in range(across):
            wrap = j == across - 1
            pieces = []
            for p in range(H // 2):
                lanes = slice(p * PAIR, (p + 1) * PAIR)
                windows = []
                for i, (own, edge) in enumerate(((k_ref, edge_k), (v_ref, edge_v))):
                    up, down = [ref.at[i * RAD : (i + 1) * RAD] for ref in (halo_up, halo_down)]
                    spans = [slice(j * SIDE, (j + 2) * SIDE)]
                    if wrap:
                        spans = [slice(cols - SIDE, cols), None, group]
                    parts = [
                        row_window(up, edge, down, block, lanes, group, beyond)
                        if span is None
                        else row_window(up, own, down, block, lanes, span, span)
                        for span in spans
                    ]
                    window = jnp.concatenate(parts, 1) if wrap else parts[0]
                    windows.append(window.reshape(-1, PAIR))
                if wrap:
                    q = jnp.concatenate(
                        [q_ref[q_rows, cols - RAD :, lanes], q_ref[q_rows, :RAD, lanes]], 1
                    )
                else:
                    q = q_ref[q_rows, j * SIDE + RAD : (j + 1) * SIDE + RAD, lanes]
                out, _, _ = softmax_pair(
                    q.reshape(SIDE * SIDE, PAIR),
                    [windows[0], gks[0][:, lanes]],
                    [windows[1], gvs[0][:, lanes]],
                    [biases[wrap], None],
                )
                pieces.append(out.astype(BF))
            done.append(jnp.concatenate(pieces, 1))
        projected = dot_nn(jnp.concatenate(done, 0), weight[...]).reshape(across, SIDE, SIDE, width)
        for j in range(across):
            before = projected[(j - 1) % across][:, RAD:]
            after = projected[j][:, :RAD]
            rows_ref[q_rows, j * SIDE : (j + 1) * SIDE, :] = jnp.concatenate([before, after], 1).astype(BF)
        band = pl.ds(block * SIDE, SIDE)
        copies.append(pltpu.make_async_copy(rows_ref.at[band], out_ref.at[band], sems.at[block]))
        copies[-1].start()
    partial_softmax(gq[...], gks, gvs, [extra_ref])
    for copy in copies:
        copy.wait()


def call(kernel, inputs, out_shapes, flops):
    specs = [pl.BlockSpec(memory_space=VMEM)] * len(inputs)
    return pl.pallas_call(
        kernel,
        out_shape=[jax.ShapeDtypeStruct(s, BF) for s in out_shapes],
        in_specs=specs,
        out_specs=[pl.BlockSpec(memory_space=VMEM)] * len(out_shapes),
        compiler_params=pltpu.CompilerParams(vmem_limit_bytes=VMEM_GRANT),
        cost_estimate=pl.CostEstimate(flops=flops, bytes_accessed=2**20, transcendentals=0),
    )(*inputs)


def body(queries, grid_keys, values, glob_queries, glob_keys, glob_values, out_weight):
    rows, cols, width = queries.shape
    own = glob_queries.shape[0]
    stations, across = lax.axis_size("station"), lax.axis_size("tm")
    chips = across // 2
    payload = width + STAT

    def over_tm(x, mask):
        return lax.ppermute(x, "tm", [(i, i ^ mask) for i in range(across)])

    def over_station(x, mask):
        return lax.ppermute(x, "station", [(i, i ^ mask) for i in range(stations)])

    up = [(i, i + 1) for i in range(stations - 1)]
    down = [(j, i) for i, j in up]
    facing = [over_tm(grid_keys, 1), over_tm(values, 1)]
    outer, glob = pl.pallas_call(
        pack_first_kernel,
        out_shape=[
            jax.ShapeDtypeStruct(shape, BF)
            for shape in [(rows, SIDE, width), (3, own, width)]
        ],
        in_specs=[pl.BlockSpec(memory_space=pltpu.HBM)] * 5,
        out_specs=[pl.BlockSpec(memory_space=VMEM)] * 2,
        scratch_shapes=[VMEM((4, rows, SIDE, width), BF), pltpu.SemaphoreType.DMA((7,))],
        compiler_params=pltpu.CompilerParams(vmem_limit_bytes=PACK_GRANT),
        cost_estimate=pl.CostEstimate(flops=10**6, bytes_accessed=2**20, transcendentals=0),
    )(grid_keys, values, glob_queries, glob_keys, glob_values)
    chip_edges = [(i, i + 1) for i in range(1, across - 1, 2)]
    outer = lax.ppermute(outer, "tm", chip_edges + [(j, i) for i, j in chip_edges])
    to_up, to_down, *edges = call(
        pack_second_kernel,
        [grid_keys, values, *facing, outer],
        [(2 * RAD, cols + SIDE, width)] * 2 + [(rows, SIDE, width)] * 2,
        10**6,
    )
    halo_up = lax.ppermute(to_up, "station", up)
    halo_down = lax.ppermute(to_down, "station", down)
    pieces = [over_tm(glob, 2 * m) for m in range(1, chips)]

    parts, arrived = [], [glob_queries, *pieces]
    for some in (arrived[: chips // 2], arrived[chips // 2 :]):
        parts += call(
            functools.partial(global_kernel, len(some)),
            [grid_keys, values, *facing, *some],
            [(own, payload)] * len(some),
            10**9,
        )
    parts = parts[:1] + [over_tm(part, 2 * m) for m, part in enumerate(parts) if m]
    merged, kv_own = call(
        functools.partial(merge_kernel, chips),
        [*parts, glob_keys, glob_values, *pieces],
        [(own, payload), (chips, 2, own, width)],
        10**8,
    )
    kv_other = over_tm(kv_own, 1)
    operands = [queries, grid_keys, values, halo_up, halo_down, kv_own, kv_other, *edges, glob_queries, out_weight]
    grid_output, extra = pl.pallas_call(
        grid_kernel,
        out_shape=[jax.ShapeDtypeStruct(s, BF) for s in ((rows, cols, width), (own, payload))],
        in_specs=[pl.BlockSpec(memory_space=VMEM)] * len(operands),
        out_specs=[pl.BlockSpec(memory_space=pltpu.HBM), pl.BlockSpec(memory_space=VMEM)],
        scratch_shapes=[VMEM((rows, cols, width), BF), pltpu.SemaphoreType.DMA((rows // SIDE,))],
        compiler_params=pltpu.CompilerParams(vmem_limit_bytes=VMEM_GRANT),
        cost_estimate=pl.CostEstimate(flops=6 * 10**9, bytes_accessed=2**20, transcendentals=0),
    )(*operands)

    parts = [merged] + [over_station(merged, m) for m in range(1, stations)]
    (glob_output,) = call(
        last_merge_kernel,
        [*parts, extra, out_weight],
        [(own, width)],
        10**8,
    )
    return grid_output, glob_output


def solution(mesh):
    return jax.shard_map(
        body,
        mesh=mesh,
        in_specs=(
            P("station", "tm", None),
            P("station", "tm", None),
            P("station", "tm", None),
            P("tm", None),
            P("tm", None),
            P("tm", None),
            P(),
        ),
        out_specs=(P("station", "tm", None), P("tm", None)),
        check_vma=False,
    )
```
